32 devices in a mesh: groups: 2 (over x), dp: 8 (over z, y), mp: 2 (over core).
Axes of the slice: x: 2, y: 2, z: 4, core: 2. Of those that a mesh axis runs over, the one named last changes fastest.
Arguments:
- residual: bfloat16 [256, 4096], P(('groups', 'dp')), parts along dimension 0, may hold values from -40 to 40
- queries: bfloat16 [256, 2048], P(('groups', 'dp'), 'mp'), parts along dimension 0, may hold values from -27 to 27
- new_kv: bfloat16 [256, 2, 2048], P(('groups', 'dp'), None, 'mp'), parts along dimension 0, may hold values from -6 to 6
- kv_pool: bfloat16 [960, 2, 16, 2048], P(('groups', 'dp'), None, None, 'mp'), parts along dimension 0, may hold values from -6 to 6
- cache_len: int32 [256], P(('groups', 'dp')), parts along dimension 0, may hold values from 24 to 47, as said below
- reconnect: int32 [64, 5], P('groups'), parts along dimension 0, may hold values from 0 to 127, as said below
- audio_tokens: int32 [256, 8], P(('groups', 'dp', 'mp')), parts along dimension 0, may hold values from 0 to 1023
- out_weight: bfloat16 [2048, 4096], P('mp'), may hold values from -0.125 to 0.125
- norm_gain: float32 [4096], replicated, may hold values from 0.1 to 1.9
- depth_in: bfloat16 [4096, 1024], P('mp'), may hold values from -0.09375 to 0.09375
- code_embed: bfloat16 [1024, 1024], replicated, may hold values from -6 to 6
- depth_gain: float32 [1024], replicated, may hold values from 0.1 to 1.9
- depth_head: bfloat16 [1024, 1024], replicated, may hold values from -0.1875 to 0.1875
Outputs:
- logits: bfloat16 [256, 8, 1024], P(('groups', 'dp', 'mp')), parts along dimension 0
- new_cache: bfloat16 [768, 2, 16, 2048], P(('groups', 'dp'), None, None, 'mp'), parts along dimension 0
The draws below stay inside these ranges and needn't reach their ends.
There are 2 independent parts, one for each index of `groups`. The reference program is written for one: setup_inputs(seed, part) draws one part's arguments, and reference() takes and returns one part's arrays. A program takes and returns all parts, laid end to end along the dimension named above; an argument that names none is the same for every part. Nothing has to cross between parts.
Inputs may be any that keep to these rules, and one draw needn't show every extreme that they name: `cache_len`: between 24 and 47; in each block of 16 sessions one session has 47 unless reset by a reconnect entry, and each holder's first listed session has 47. `reconnect`: row r: session, holding index of dp, owner index of dp (session // 16), page count ceil(cache_len of the session / 16) (up to 3, reached at every holder), first pool page local to the holder, equal to 48 + k * 3 for the holder's k-th entry. Holder differs from owner; each holder lists 4 sessions of distinct owners; a session appears at most once.
All inputs are finite; a program needn't handle non-finite values.
Results may differ from the reference program's by a relative error of at most 0.006.
Values may be sent and summed in bfloat16 or wider, within the bound.
A program may use at most 128 MiB of HBM per device.

```python
import jax
import jax.numpy as jnp
from jax import lax

D = 4096
HEADS = 16
HD = 128
DD = 1024
VOCAB = 1024
NCB = 8
PAGE = 16
PAGES = 3
SESS_DEV = 8
CTX = 48
SESSIONS = 128
POOL_DEV = 60
N_DP = 8
N_MP = 2


def session_plan(key):
    per_block = SESS_DEV * N_MP
    session_count = per_block * N_DP
    held_count = N_DP // 2
    len_key, score_key, pop_key, perm_key = jax.random.split(key, 4)
    lengths = CTX - 1 - jax.random.randint(len_key, (session_count,), 0, CTX // 2)
    within = jnp.arange(session_count) % per_block
    lengths = jnp.where(within == 0, CTX - 1, lengths)
    lengths = jnp.where(within == 1, CTX // 2, lengths)
    popular = jax.random.permutation(pop_key, N_DP) < 3
    base_score = jax.random.randint(score_key, (N_DP, N_DP), 0, 65536)
    scores = (base_score + jnp.where(popular, 131072, 0)[None, :]) * N_DP + jnp.arange(N_DP)[None, :]
    scores = jnp.where(jnp.arange(N_DP)[:, None] == jnp.arange(N_DP)[None, :], -1, scores)
    chosen = lax.top_k(scores.astype(jnp.int32), held_count)[1]
    owner_ids = chosen.reshape(-1).astype(jnp.int32)
    holder_ids = jnp.repeat(jnp.arange(N_DP), held_count).astype(jnp.int32)
    entry_slot = jnp.tile(jnp.arange(held_count), N_DP).astype(jnp.int32)
    onehot = (owner_ids[:, None] == jnp.arange(N_DP)[None, :]).astype(jnp.int32)
    entry_rank = jnp.sum((jnp.cumsum(onehot, 0) - onehot) * onehot, 1)
    orders = jax.vmap(lambda sub_key: jax.random.permutation(sub_key, per_block))(jax.random.split(perm_key, N_DP))
    local_ids = orders[owner_ids, entry_rank]
    session_ids = owner_ids * per_block + local_ids
    lengths = lengths.at[session_ids].set(jnp.where(entry_slot == 0, CTX - 1, lengths[session_ids]))
    page_total = (lengths[session_ids] + PAGE - 1) // PAGE
    first_page = per_block * PAGES + entry_slot * PAGES
    entries = jnp.stack([session_ids, holder_ids, owner_ids, page_total, first_page], 1).astype(jnp.int32)
    return (lengths.astype(jnp.int32), entries)


def draw_cache_len(key, part):
    return session_plan(key)[0]


def draw_reconnect(key, part):
    return session_plan(key)[1]


def draw_queries(key, part):
    key = jax.random.fold_in(key, 21)
    noise_key = jax.random.fold_in(key, 0)
    noise = jax.random.truncated_normal(noise_key, -6.0, 6.0, (SESSIONS, HEADS * HD))
    return noise.astype(jnp.bfloat16)


def draw_new_kv(key, part):
    key = jax.random.fold_in(key, 22)
    noise = jax.random.truncated_normal(key, -6.0, 6.0, (SESSIONS, 2, HEADS * HD))
    return noise.astype(jnp.bfloat16)


def draw_kv_pool(key, part):
    key = jax.random.fold_in(key, 23)
    noise = jax.random.truncated_normal(key, -6.0, 6.0, (N_DP * POOL_DEV, 2, PAGE, HEADS * HD))
    return noise.astype(jnp.bfloat16)


def draw_residual(key, part):
    key = jax.random.fold_in(key, 24)
    noise_key = jax.random.fold_in(key, 0)
    noise = jax.random.truncated_normal(noise_key, -4.0, 4.0, (SESSIONS, D))
    return noise.astype(jnp.bfloat16)


def with_ends(drawn, stream_key, smallest, high):
    index_at = [jax.random.randint(jax.random.fold_in(stream_key, axis), (), 0, length) for axis, length in enumerate(drawn.shape)]
    longest = drawn.shape.index(max(drawn.shape))
    next_to = index_at[:longest] + [(index_at[longest] + 1) % drawn.shape[longest]] + index_at[longest + 1:]
    return drawn.at[tuple(index_at)].set(smallest).at[tuple(next_to)].set(high)


def block_levels(own_key, shape, pieces, low, top_value):
    loudness, own = 1.0, jax.random.fold_in(own_key, 6)
    for dim, parts in pieces:
        steps = jnp.exp(jax.random.uniform(jax.random.fold_in(own, dim), (parts,), jnp.float32, low / len(pieces), top_value / len(pieces)))
        loudness = loudness * jnp.repeat(steps, shape[dim] // parts).reshape([-1 if axis == dim else 1 for axis in range(len(shape))])
    return loudness


def normal_values(key, dims, scale, bound, shards=(), held_as=jnp.bfloat16):
    values = jax.random.normal(key, dims, jnp.float32) * scale
    if len(shards) > 0:
        values = block_levels(key, dims, shards, -0.22, 0.18) * values
    return jnp.clip(values, min=-bound, max=bound).astype(held_as)


def setup_inputs(seed: int = 0, part: int = 0) -> dict:
    streams_of = jax.random.split(jax.random.key(seed), 14)
    part_splits = jax.random.split(jax.random.fold_in(streams_of[13], part), 14)
    return {
        "residual": draw_residual(jax.random.fold_in(jax.random.fold_in(streams_of[13], part), 71), part),
        "queries": draw_queries(jax.random.fold_in(jax.random.fold_in(streams_of[13], part), 71), part),
        "new_kv": draw_new_kv(jax.random.fold_in(jax.random.fold_in(streams_of[13], part), 71), part),
        "kv_pool": draw_kv_pool(jax.random.fold_in(jax.random.fold_in(streams_of[13], part), 71), part),
        "cache_len": draw_cache_len(jax.random.fold_in(jax.random.fold_in(streams_of[13], part), 71), part),
        "reconnect": draw_reconnect(jax.random.fold_in(jax.random.fold_in(streams_of[13], part), 71), part),
        "audio_tokens": with_ends(jax.random.randint(part_splits[6], (SESSIONS, NCB), 0, VOCAB), jax.random.fold_in(part_splits[6], 1), 0, VOCAB - 1).astype(jnp.int32),
        "out_weight": normal_values(streams_of[7], (HEADS * HD, D), (HEADS * HD) ** -0.5, 0.125, ((0, 2),)),
        "norm_gain": jnp.clip(1.0 + 0.18 * jax.random.normal(streams_of[8], (D,), jnp.float32), 0.1, 1.9),
        "depth_in": normal_values(streams_of[9], (D, DD), D ** -0.5, 0.09375, ((0, 2),)),
        "code_embed": normal_values(streams_of[10], (VOCAB, DD), 1.0, 6.0),
        "depth_gain": jnp.clip(1.0 + 0.18 * jax.random.normal(streams_of[11], (DD,), jnp.float32), 0.1, 1.9),
        "depth_head": normal_values(streams_of[12], (DD, VOCAB), DD ** -0.5, 0.1875),
    }


def attend(queries, kv_pages, lengths):
    batch_size, page_count, _, page_size, feature_width = kv_pages.shape
    head_count = feature_width // HD
    context_span = page_count * page_size
    key_rows = kv_pages[:, :, 0].reshape(batch_size, context_span, head_count, HD).astype(jnp.float32)
    value_rows = kv_pages[:, :, 1].reshape(batch_size, context_span, head_count, HD).astype(jnp.float32)
    query_heads = queries.reshape(batch_size, head_count, HD).astype(jnp.float32)
    scores = jnp.einsum('bhd,bthd->bht', query_heads, key_rows) * HD ** (-0.5)
    position = jnp.arange(context_span, dtype=jnp.int32)
    visible = position[None, None, :] <= lengths[:, None, None]
    highest = lax.optimization_barrier(jnp.max(jnp.where(visible, scores, -jnp.inf), -1, keepdims=True))
    weights = jnp.where(visible, jnp.exp(scores - highest), 0.0)
    weights = (weights / lax.optimization_barrier(jnp.sum(weights, -1, keepdims=True))).astype(jnp.bfloat16)
    mixture = jnp.einsum('bht,bthd->bhd', weights.astype(jnp.float32), value_rows)
    return mixture.reshape(batch_size, feature_width).astype(jnp.bfloat16)

def write_new(kv_pages, new_kv, lengths):
    page_count, page_size = (kv_pages.shape[1], kv_pages.shape[3])
    position = jnp.arange(page_count, dtype=jnp.int32)[:, None] * page_size + jnp.arange(page_size, dtype=jnp.int32)[None, :]
    landed = position[None, :, :] == lengths[:, None, None]
    return jnp.where(landed[:, :, None, :, None], new_kv[:, None, :, None, :], kv_pages)

def reference(residual, queries, new_kv, kv_pool, cache_len, reconnect, audio_tokens, out_weight, norm_gain, depth_in, code_embed, depth_gain, depth_head):
    session_count = cache_len.shape[0]
    per_block = session_count // N_DP
    session_ids = jnp.arange(session_count, dtype=jnp.int32)
    owner_ids = session_ids // per_block
    local_ids = session_ids % per_block
    page_ids = jnp.arange(PAGES, dtype=jnp.int32)
    home_slot = (owner_ids * POOL_DEV + local_ids * PAGES)[:, None] + page_ids[None, :]
    matched = (session_ids[:, None] == reconnect[None, :, 0]).astype(jnp.int32)
    linked = lax.optimization_barrier(jnp.sum(matched, 1)) > 0
    holder = lax.optimization_barrier(jnp.sum(matched * reconnect[None, :, 1], 1))
    page_total = lax.optimization_barrier(jnp.sum(matched * reconnect[None, :, 3], 1))
    first_page = lax.optimization_barrier(jnp.sum(matched * reconnect[None, :, 4], 1))
    remote = (holder * POOL_DEV + first_page)[:, None] + page_ids[None, :]
    source = jnp.where(linked[:, None], remote, home_slot).astype(jnp.int32)
    kv_pages = kv_pool[source]
    keeping = jnp.logical_or(jnp.logical_not(linked)[:, None], page_ids[None, :] < page_total[:, None])
    kv_pages = jnp.where(keeping[:, :, None, None, None], kv_pages, jnp.zeros((), kv_pages.dtype))
    kv_pages = write_new(kv_pages, new_kv, cache_len)
    new_cache = kv_pages.reshape((session_count * PAGES,) + kv_pool.shape[1:])
    attention = attend(queries, kv_pages, cache_len)
    summed = jnp.dot(attention, out_weight, preferred_element_type=jnp.float32)
    layer_out = (residual.astype(jnp.float32) + summed).astype(jnp.bfloat16)
    layer_out = lax.optimization_barrier(layer_out).astype(jnp.float32)
    inverse_rms = lax.rsqrt(lax.optimization_barrier(jnp.mean(layer_out * layer_out, 1, keepdims=True)) + 1e-05)
    normed = (layer_out * inverse_rms * norm_gain).astype(jnp.bfloat16)
    lifted = jnp.dot(normed, depth_in, preferred_element_type=jnp.float32)
    embedded = code_embed[audio_tokens].astype(jnp.float32)
    hidden = lifted[:, None, :] + embedded
    depth_rms = lax.rsqrt(lax.optimization_barrier(jnp.mean(hidden * hidden, -1, keepdims=True)) + 1e-05)
    depth_normed = (hidden * depth_rms * depth_gain).astype(jnp.bfloat16)
    logits = jnp.dot(depth_normed.reshape(-1, hidden.shape[-1]), depth_head, preferred_element_type=jnp.float32)
    return (logits.astype(jnp.bfloat16).reshape(audio_tokens.shape + (depth_head.shape[1],)), new_cache)
```

```python
import functools

import jax
import jax.numpy as jnp
from jax import lax
from jax.experimental import pallas as pl
from jax.experimental.pallas import tpu as pltpu
from jax.sharding import PartitionSpec as P

HD = 128
PAGES = 3
GROUP = 8
COLS = 512
EARLY = 7
F32 = jnp.float32
BF16 = jnp.bfloat16
MESH = pl.DeviceIdType.MESH


def iota(shape, dim):
    return lax.broadcasted_iota(jnp.int32, shape, dim)


def attend_group(pages_of, q8s, k8s, v8s, lens):
    heads = q8s[0].shape[0]
    width = heads * HD
    own = (iota((heads, width), 1) // HD) == iota((heads, width), 0)
    scores, heres = [], []
    for j in range(len(q8s)):
        keys = jnp.concatenate([pages_of(j, p, 0) for p in range(PAGES)], axis=0)
        place = iota((heads, keys.shape[0]), 1)
        spread = jnp.where(own, jnp.concatenate([q8s[j]] * heads, axis=1), 0.0).astype(BF16)
        s = lax.dot_general(spread, keys, (((1,), (1,)), ((), ())), preferred_element_type=F32)
        s = s * HD ** (-0.5)
        fresh = jnp.sum(q8s[j] * k8s[j], axis=1, keepdims=True) * HD ** (-0.5)
        here = place == lens[j]
        s = jnp.where(here, fresh, s)
        scores.append(jnp.where(place <= lens[j], s, -jnp.inf))
        heres.append(here)
    s = jnp.concatenate(scores, axis=0)
    e = jnp.exp(s - jnp.max(s, axis=1, keepdims=True))
    w = (e / jnp.sum(e, axis=1, keepdims=True)).astype(BF16).astype(F32)
    row = iota((heads, HD), 0)
    results = []
    for j in range(len(q8s)):
        mine = w[j * heads:(j + 1) * heads]
        values = jnp.concatenate([pages_of(j, p, 1) for p in range(PAGES)], axis=0)
        old = jnp.where(heres[j], 0.0, mine).astype(BF16)
        mixed = jnp.dot(old, values, preferred_element_type=F32)
        total = jnp.sum(jnp.where(heres[j], mine, 0.0), axis=1, keepdims=True) * v8s[j]
        for h in range(heads):
            total = total + jnp.where(row == h, mixed[:, h * HD:(h + 1) * HD], 0.0)
        results.append(total)
    return results


def main_kernel(n, rec, lens, rec_t, len_row, qkv, residual, tokens, norm_gain, depth_gain,
                pool, out_w, depth_in, code_embed, depth_head,
                inbound, logits,
                held, outbound, resident, ow_v, di_v, ce_v, dh_v,
                qkv3, msg32, msg, msg_in, rep, rep_in, local,
                po_send, po_mine, po_in, ss_send, ss_in, lf, lf_in, emb, base_s,
                held_sem, load_sem, msg_ss, msg_rs, page_ss, page_rs, rep_ss, rep_rs, mp_ss, mp_rs):
    g, me, m = lax.axis_index("groups"), lax.axis_index("dp"), lax.axis_index("mp")
    sessions = residual.shape[0]
    width = qkv.shape[1] // 3
    heads = width // HD
    homes = sessions * PAGES
    rows = rec_t.shape[1]
    half = residual.shape[1] // 2
    features = residual.shape[1]

    load_held = pltpu.make_async_copy(pool.at[pl.ds(homes, held.shape[0])], held, held_sem)
    load_held.start()

    def peer(shift):
        return (g, lax.rem(me + shift + n, n), m)

    partner = (g, me, 1 - m)
    barrier = pltpu.get_barrier_semaphore()
    for s in range(1, n):
        pl.semaphore_signal(barrier, inc=1, device_id=peer(s), device_id_type=MESH)
    pl.semaphore_signal(barrier, inc=1, device_id=partner, device_id_type=MESH)

    session, holder = rec_t[0:1, :], rec_t[1:2, :]
    behind = me - holder
    behind = jnp.where(behind < 0, behind + n, behind)
    is_session = jnp.where(session == iota((sessions, rows), 0) + me * sessions, 1.0, 0.0).astype(BF16)
    is_slot = jnp.where(behind == iota((n, rows), 0), 1.0, 0.0).astype(BF16)
    nt = (((1,), (1,)), ((), ()))
    pair = lax.dot_general(is_session, is_slot, nt, preferred_element_type=F32)
    pair_t = lax.dot_general(is_slot, is_session, nt, preferred_element_type=F32).astype(BF16)
    eye = iota((sessions, sessions), 0) == iota((sessions, sessions), 1)
    len_col = jnp.sum(jnp.where(eye, len_row[...].astype(F32), 0.0), axis=1, keepdims=True)
    len_wide = jnp.broadcast_to(len_col, (sessions, HD)).astype(BF16)
    sent = jnp.dot(pair_t, qkv[...], preferred_element_type=F32)
    sent_len = jnp.dot(pair_t, len_wide, preferred_element_type=F32)
    for c in range(3 * heads):
        msg32[:, c, :] = sent[:, c * HD:(c + 1) * HD]
    for c in range(heads):
        msg32[:, 3 * heads + c, :] = sent_len
    msg[...] = msg32[...].astype(BF16)

    def find(r, bases):
        ahead = rec[r, 2] - me
        ahead = jnp.where(ahead < 0, ahead + n, ahead)
        ahead = jnp.where(rec[r, 1] == me, ahead, -1)
        first = rec[r, 4] - homes
        return tuple(jnp.where(ahead == s, first, b) for s, b in enumerate(bases))

    bases = lax.fori_loop(0, rows, find, tuple(jnp.int32(0) for _ in range(n)))
    for s in range(n):
        base_s[s] = jnp.clip(bases[s], 0, held.shape[0] - PAGES)

    pl.semaphore_wait(barrier, n)
    msgs, pages, reps = [], [], []
    for s in range(1, n):
        c = pltpu.make_async_remote_copy(msg.at[s], msg_in.at[s], msg_ss.at[s], msg_rs.at[s],
                                         device_id=peer(-s), device_id_type=MESH)
        c.start()
        msgs.append(c)
        pages.append(pltpu.make_async_remote_copy(
            outbound.at[s], inbound.at[s], page_ss.at[s], page_rs.at[s],
            device_id=peer(s), device_id_type=MESH))
        reps.append(pltpu.make_async_remote_copy(
            rep.at[s], rep_in.at[s], rep_ss.at[s], rep_rs.at[s],
            device_id=peer(s), device_id_type=MESH))
    load_held.wait()
    for s in range(n):
        for p in range(PAGES):
            outbound[s, p] = held[base_s[s] + p]
        if 1 <= s <= EARLY:
            pages[s - 1].start()

    loads = [
        pltpu.make_async_copy(src, dst, load_sem.at[i])
        for i, (src, dst) in enumerate([
            (pool.at[pl.ds(0, homes)], resident), (out_w, ow_v), (depth_in, di_v),
            (code_embed, ce_v), (depth_head, dh_v)])
    ]
    for c in loads:
        c.start()

    wide = qkv[...].astype(F32)
    for c in range(3 * heads):
        qkv3[:, c, :] = wide[:, c * HD:(c + 1) * HD]
    msg_in[0] = jnp.zeros_like(msg_in[0])
    rep_in[0] = jnp.zeros_like(rep_in[0])

    for c in msgs:
        c.wait_recv()

    @pl.loop(0, n // GROUP)
    def _(t):
        at = [t * GROUP + j for j in range(GROUP)]
        got = [msg_in[a].astype(F32) for a in at]
        out = attend_group(
            lambda j, p, kv: outbound[at[j], p, kv],
            [x[0:heads] for x in got], [x[heads:2 * heads] for x in got],
            [x[2 * heads:3 * heads] for x in got],
            [x[3 * heads:4 * heads, 0:1].astype(jnp.int32) for x in got])
        for j in range(GROUP):
            rep[at[j]] = out[j]

    for c in reps:
        c.start()
    for s in range(EARLY + 1, n):
        pages[s - 1].start()

    loads[0].wait()

    @pl.loop(0, sessions // GROUP)
    def _(t):
        at = [t * GROUP + j for j in range(GROUP)]
        got = [qkv3[a] for a in at]
        out = attend_group(
            lambda j, p, kv: resident[at[j] * PAGES + p, kv],
            [x[0:heads] for x in got], [x[heads:2 * heads] for x in got],
            [x[2 * heads:3 * heads] for x in got], [lens[a] for a in at])
        for j in range(GROUP):
            local[at[j]] = out[j]

    loads[3].wait()
    count, books = tokens.shape
    entries = code_embed.shape[0]
    diag = iota((books, books), 0) == iota((books, books), 1)
    picks = []
    for b in range(count):
        col = jnp.sum(jnp.where(diag, tokens[b:b + 1, :].astype(F32), 0.0), axis=1, keepdims=True)
        hit = col.astype(jnp.int32) == iota((books, entries), 1)
        picks.append(jnp.where(hit, 1.0, 0.0))
    pick = jnp.concatenate(picks, axis=0).astype(BF16)

    @pl.loop(0, emb.shape[1] // COLS)
    def _(t):
        at = pl.ds(pl.multiple_of(t * COLS, COLS), COLS)
        emb[:, at] = jnp.dot(pick, ce_v[:, at], preferred_element_type=F32)

    for c in reps:
        c.wait_recv()
    here = jnp.concatenate([local[:, h, :] for h in range(heads)], axis=1)
    away = jnp.concatenate([rep_in[:, h, :] for h in range(heads)], axis=1).astype(BF16)
    away = jnp.dot(pair.astype(BF16), away, preferred_element_type=F32)
    linked = jnp.sum(pair, axis=1, keepdims=True) > 0.0
    attention = jnp.where(linked, away, here).astype(BF16)

    loads[1].wait()

    def project(first, target):
        @pl.loop(0, half // COLS)
        def _(t):
            at = pl.ds(pl.multiple_of(first + t * COLS, COLS), COLS)
            to = pl.ds(pl.multiple_of(t * COLS, COLS), COLS)
            target[:, to] = jnp.dot(attention, ow_v[:, at], preferred_element_type=F32)

    def swap(i, src, dst):
        c = pltpu.make_async_remote_copy(src, dst, mp_ss.at[i], mp_rs.at[i],
                                         device_id=partner, device_id_type=MESH)
        c.start()
        return c

    project((1 - m) * half, po_send)
    swap0 = swap(0, po_send, po_in)
    project(m * half, po_mine)
    swap0.wait_recv()
    my_half = pl.ds(pl.multiple_of(m * half, half), half)
    layer = residual[:, my_half].astype(F32) + (po_mine[...] + po_in[...])
    layer = layer.astype(BF16).astype(F32)
    squares = jnp.sum(layer * layer, axis=1, keepdims=True)
    ss_send[...] = jnp.broadcast_to(squares, ss_send.shape)
    swap1 = swap(1, ss_send, ss_in)
    loads[2].wait()
    swap1.wait_recv()
    squares = squares + ss_in[:, 0:1]
    normed = (layer * lax.rsqrt(squares * (1.0 / features) + 1e-05) * norm_gain[:, my_half]).astype(BF16)
    for t in range(lf.shape[1] // COLS):
        at = slice(t * COLS, (t + 1) * COLS)
        lf[:, at] = jnp.dot(normed, di_v[:, at], preferred_element_type=F32)
    swap2 = swap(2, lf.at[pl.ds(pl.multiple_of((1 - m) * count, count), count)], lf_in)
    loads[4].wait()
    swap2.wait_recv()
    lifted = lf[pl.ds(pl.multiple_of(m * count, count), count), :] + lf_in[...]
    parts = []
    for b in range(count):
        hidden = lifted[b:b + 1, :] + emb[b * books:(b + 1) * books, :]
        mean = jnp.mean(hidden * hidden, axis=1, keepdims=True)
        parts.append(hidden * lax.rsqrt(mean + 1e-05) * depth_gain[...])
    depth_normed = jnp.concatenate(parts, axis=0).astype(BF16)
    for t in range(logits.shape[1] // COLS):
        at = slice(t * COLS, (t + 1) * COLS)
        logits[:, at] = jnp.dot(depth_normed, dh_v[:, at], preferred_element_type=F32).astype(BF16)

    for c in (swap0, swap1, swap2):
        c.wait_send()
    for c in msgs + reps:
        c.wait_send()
    for c in pages:
        c.wait_send()
    for c in pages:
        c.wait_recv()


def place_kernel(n, rec, lens, qkv, pool, inbound, logits_in, cache, logits, buf, slot, pages,
                 in_sem, out_sem, log_sem):
    me = lax.axis_index("dp")
    sessions = qkv.shape[0]
    width = qkv.shape[1] // 3
    copy_logits = pltpu.make_async_copy(logits_in, logits, log_sem)
    copy_logits.start()
    for i in range(sessions):
        slot[i] = 0

    @pl.loop(0, rec.shape[0])
    def _(r):
        @pl.when(rec[r, 2] == me)
        def _():
            behind = me - rec[r, 1]
            i = rec[r, 0] - me * sessions
            slot[i] = jnp.where(behind < 0, behind + n, behind)
            pages[i] = rec[r, 3]

    def space(i):
        return buf.at[pl.ds(i * PAGES, PAGES)]

    @pl.loop(0, sessions)
    def _(i):
        @pl.when(slot[i] == 0)
        def _():
            pltpu.make_async_copy(pool.at[pl.ds(i * PAGES, PAGES)], space(i), in_sem.at[i]).start()

        @pl.when(slot[i] != 0)
        def _():
            pltpu.make_async_copy(inbound.at[slot[i]], space(i), in_sem.at[i]).start()

    def give(i):
        return pltpu.make_async_copy(space(i), cache.at[pl.ds(i * PAGES, PAGES)], out_sem.at[i])

    for i in range(sessions):
        pltpu.make_async_copy(pool.at[pl.ds(i * PAGES, PAGES)], space(i), in_sem.at[i]).wait()

        @pl.when(slot[i] != 0)
        def _():
            for p in range(PAGES):
                @pl.when(p >= pages[i])
                def _():
                    buf[i * PAGES + p] = jnp.zeros(buf.shape[1:], BF16)

        size = buf.shape[2]
        page = i * PAGES + lens[i] // size
        hit = iota((size, width), 0) == lax.rem(lens[i], size)
        for kv in range(2):
            new = qkv[:, (1 + kv) * width:(2 + kv) * width].astype(F32)[i:i + 1, :]
            buf[page, kv] = jnp.where(hit, new, buf[page, kv].astype(F32)).astype(BF16)
        give(i).start()
    for i in range(sessions):
        give(i).wait()
    copy_logits.wait()


def on_device(n, residual, queries, new_kv, kv_pool, cache_len, reconnect, audio_tokens, out_weight,
              norm_gain, depth_in, code_embed, depth_gain, depth_head):
    sessions, width = queries.shape
    heads = width // HD
    qkv = jnp.concatenate([queries, new_kv.reshape(sessions, 2 * width)], axis=1)
    count, books = audio_tokens.shape
    page = kv_pool.shape[1:]
    homes = sessions * PAGES
    features = residual.shape[1]
    half = features // 2
    depth = depth_in.shape[1]
    entries = depth_head.shape[1]
    vmem = pl.BlockSpec(memory_space=pltpu.VMEM)
    smem = pl.BlockSpec(memory_space=pltpu.SMEM)
    anywhere = pl.BlockSpec(memory_space=pl.ANY)
    dma = pltpu.SemaphoreType.DMA
    inbound, logits = pl.pallas_call(
        functools.partial(main_kernel, n),
        out_shape=(jax.ShapeDtypeStruct((n, PAGES) + page, BF16),
                   jax.ShapeDtypeStruct((count * books, entries), BF16)),
        in_specs=[smem, smem] + [vmem] * 7 + [anywhere] * 5,
        out_specs=(anywhere, vmem),
        scratch_shapes=[
            pltpu.VMEM((kv_pool.shape[0] - homes,) + page, BF16),
            pltpu.VMEM((n, PAGES) + page, BF16),
            pltpu.VMEM((homes,) + page, BF16),
            pltpu.VMEM(out_weight.shape, BF16),
            pltpu.VMEM(depth_in.shape, BF16),
            pltpu.VMEM(code_embed.shape, BF16),
            pltpu.VMEM(depth_head.shape, BF16),
            pltpu.VMEM((sessions, 3 * heads, HD), F32),
            pltpu.VMEM((n, 4 * heads, HD), F32),
            pltpu.VMEM((n, 4 * heads, HD), BF16),
            pltpu.VMEM((n, 4 * heads, HD), BF16),
            pltpu.VMEM((n, heads, HD), F32),
            pltpu.VMEM((n, heads, HD), F32),
            pltpu.VMEM((sessions, heads, HD), F32),
            pltpu.VMEM((sessions, half), F32),
            pltpu.VMEM((sessions, half), F32),
            pltpu.VMEM((sessions, half), F32),
            pltpu.VMEM((sessions, HD), F32),
            pltpu.VMEM((sessions, HD), F32),
            pltpu.VMEM((sessions, depth), F32),
            pltpu.VMEM((count, depth), F32),
            pltpu.VMEM((count * books, depth), F32),
            pltpu.SMEM((n,), jnp.int32),
            dma, dma((5,)), dma((n,)), dma((n,)), dma((n,)), dma((n,)), dma((n,)), dma((n,)),
            dma((3,)), dma((3,)),
        ],
        compiler_params=pltpu.CompilerParams(
            collective_id=0, has_side_effects=True, vmem_limit_bytes=48 * 1024 * 1024),
        name="serve",
    )(reconnect, cache_len, reconnect.T, cache_len.reshape(1, sessions), qkv, residual, audio_tokens,
      norm_gain.reshape(1, features), depth_gain.reshape(1, depth),
      kv_pool, out_weight, depth_in, code_embed, depth_head)
    new_cache, logits = pl.pallas_call(
        functools.partial(place_kernel, n),
        out_shape=(jax.ShapeDtypeStruct((homes,) + page, BF16),
                   jax.ShapeDtypeStruct((count * books, entries), BF16)),
        in_specs=[smem, smem, vmem, anywhere, anywhere, anywhere],
        out_specs=(anywhere, anywhere),
        scratch_shapes=[
            pltpu.VMEM((homes,) + page, BF16),
            pltpu.SMEM((sessions,), jnp.int32),
            pltpu.SMEM((sessions,), jnp.int32),
            dma((sessions,)), dma((sessions,)), dma,
        ],
        compiler_params=pltpu.CompilerParams(vmem_limit_bytes=32 * 1024 * 1024),
        name="place",
    )(reconnect, cache_len, qkv, kv_pool, inbound, logits)
    return (logits.reshape(count, books, entries), new_cache)


def solution(mesh):
    in_specs = (
        P(("groups", "dp"), None),
        P(("groups", "dp"), "mp"),
        P(("groups", "dp"), None, "mp"),
        P(("groups", "dp"), None, None, "mp"),
        P(("groups", "dp")),
        P("groups", None),
        P(("groups", "dp", "mp"), None),
        P("mp", None),
        P(),
        P("mp", None),
        P(),
        P(),
        P(),
    )
    out_specs = (P(("groups", "dp", "mp"), None, None), P(("groups", "dp"), None, None, "mp"))
    return jax.shard_map(
        functools.partial(on_device, mesh.shape["dp"]), mesh=mesh, in_specs=in_specs,
        out_specs=out_specs, check_vma=False
    )
```

```python
import functools

import jax
import jax.numpy as jnp
from jax import lax
from jax.experimental import pallas as pl
from jax.experimental.pallas import tpu as pltpu
from jax.sharding import PartitionSpec as P

HD = 128
PAGES = 3
GROUP = 8
COLS = 512
EARLY = 2
F32 = jnp.float32
BF16 = jnp.bfloat16
MESH = pl.DeviceIdType.MESH


def iota(shape, dim):
    return lax.broadcasted_iota(jnp.int32, shape, dim)


def attend_group(pages_of, q8s, k8s, v8s, lens):
    heads = q8s[0].shape[0]
    width = heads * HD
    own = (iota((heads, width), 1) // HD) == iota((heads, width), 0)
    scores, heres = [], []
    for j in range(len(q8s)):
        keys = jnp.concatenate([pages_of(j, p, 0) for p in range(PAGES)], axis=0)
        place = iota((heads, keys.shape[0]), 1)
        spread = jnp.where(own, jnp.concatenate([q8s[j]] * heads, axis=1), 0.0).astype(BF16)
        s = lax.dot_general(spread, keys, (((1,), (1,)), ((), ())), preferred_element_type=F32)
        s = s * HD ** (-0.5)
        fresh = jnp.sum(q8s[j] * k8s[j], axis=1, keepdims=True) * HD ** (-0.5)
        here = place == lens[j]
        s = jnp.where(here, fresh, s)
        scores.append(jnp.where(place <= lens[j], s, -jnp.inf))
        heres.append(here)
    s = jnp.concatenate(scores, axis=0)
    e = jnp.exp(s - jnp.max(s, axis=1, keepdims=True))
    w = (e / jnp.sum(e, axis=1, keepdims=True)).astype(BF16).astype(F32)
    row = iota((heads, HD), 0)
    results = []
    for j in range(len(q8s)):
        mine = w[j * heads:(j + 1) * heads]
        values = jnp.concatenate([pages_of(j, p, 1) for p in range(PAGES)], axis=0)
        old = jnp.where(heres[j], 0.0, mine).astype(BF16)
        mixed = jnp.dot(old, values, preferred_element_type=F32)
        total = jnp.sum(jnp.where(heres[j], mine, 0.0), axis=1, keepdims=True) * v8s[j]
        for h in range(heads):
            total = total + jnp.where(row == h, mixed[:, h * HD:(h + 1) * HD], 0.0)
        results.append(total)
    return results


def settle(cache, pages, h, length, new, count):
    size, width = cache.shape[2:]
    for p, at in enumerate(pages):
        old = cache[at, h].astype(F32)
        if count is not None:
            old = jnp.where(p < count, old, 0.0)
        hit = iota((size, width), 0) + p * size == length
        cache[at, h] = jnp.where(hit, new, old).astype(BF16)


def main_kernel(n, rec, lens, *refs):
    small_in, (pool, out_w, depth_in, code_embed, depth_head), (inbound, resident, logits) = (
        refs[:8], refs[8:13], refs[13:16])
    rec_t, len_row, queries, kv, residual, tokens, norm_gain, depth_gain = small = refs[16:24]
    run_main(n, rec, lens, rec_t, len_row, queries, kv, residual, tokens, norm_gain, depth_gain,
             pool, out_w, depth_in, code_embed, depth_head, inbound, resident, logits,
             small_in, small, *refs[24:])


def run_main(n, rec, lens, rec_t, len_row, queries, kv, residual, tokens, norm_gain, depth_gain,
                pool, out_w, depth_in, code_embed, depth_head,
                inbound, resident, logits, small_in, small,
                held, outbound, ow_v, di_v, ce_v, dh_v, kv32, sent_kv, sent_len_v, small_sem,
                qkv3, msg32, msg, msg_in, rep, rep_in, local,
                po_send, po_mine, po_in, ss_send, ss_in, lf, lf_in, emb, base_s,
                held_sem, load_sem, msg_ss, msg_rs, page_ss, page_rs, rep_ss, rep_rs, mp_ss, mp_rs):
    g, me, m = lax.axis_index("groups"), lax.axis_index("dp"), lax.axis_index("mp")
    sessions = residual.shape[0]
    width = queries.shape[1]
    heads = width // HD
    homes = sessions * PAGES
    rows = rec_t.shape[1]
    half = residual.shape[1] // 2
    features = residual.shape[1]

    load_held = pltpu.make_async_copy(pool.at[pl.ds(homes, held.shape[0])], held, held_sem)
    load_held.start()
    fetch = [pltpu.make_async_copy(src, dst, small_sem.at[i])
             for i, (src, dst) in enumerate(zip(small_in, small))]
    for c in fetch:
        c.start()

    def peer(shift):
        return (g, lax.rem(me + shift + n, n), m)

    partner = (g, me, 1 - m)
    barrier = pltpu.get_barrier_semaphore()
    for s in range(1, n):
        pl.semaphore_signal(barrier, inc=1, device_id=peer(s), device_id_type=MESH)
    pl.semaphore_signal(barrier, inc=1, device_id=partner, device_id_type=MESH)

    for c in fetch:
        c.wait()
    kv32[...] = kv[...].astype(F32)

    session, holder = rec_t[0:1, :], rec_t[1:2, :]
    behind = me - holder
    behind = jnp.where(behind < 0, behind + n, behind)
    is_session = jnp.where(session == iota((sessions, rows), 0) + me * sessions, 1.0, 0.0).astype(BF16)
    is_slot = jnp.where(behind == iota((n, rows), 0), 1.0, 0.0).astype(BF16)
    nt = (((1,), (1,)), ((), ()))
    pair = lax.dot_general(is_session, is_slot, nt, preferred_element_type=F32)
    pair_t = lax.dot_general(is_slot, is_session, nt, preferred_element_type=F32).astype(BF16)
    eye = iota((sessions, sessions), 0) == iota((sessions, sessions), 1)
    len_col = jnp.sum(jnp.where(eye, len_row[...].astype(F32), 0.0), axis=1, keepdims=True)
    len_wide = jnp.broadcast_to(len_col, (sessions, HD)).astype(BF16)
    sent = jnp.concatenate(
        [jnp.dot(pair_t, x, preferred_element_type=F32)
         for x in (queries[...], kv32[:, 0, :].astype(BF16), kv32[:, 1, :].astype(BF16))], axis=1)
    sent_kv[...] = sent[:, width:]
    sent_len_v[...] = sent_len = jnp.dot(pair_t, len_wide, preferred_element_type=F32)
    for c in range(3 * heads):
        msg32[:, c, :] = sent[:, c * HD:(c + 1) * HD]
    for c in range(heads):
        msg32[:, 3 * heads + c, :] = sent_len
    msg[...] = msg32[...].astype(BF16)

    def find(r, bases):
        ahead = rec[2, r] - me
        ahead = jnp.where(ahead < 0, ahead + n, ahead)
        ahead = jnp.where(rec[1, r] == me, ahead, -1)
        first = rec[4, r] - homes
        return tuple(jnp.where(ahead == s, first, b) for s, b in enumerate(bases))

    bases = lax.fori_loop(0, rows, find, tuple(jnp.int32(0) for _ in range(n)))
    for s in range(n):
        base_s[s] = jnp.clip(bases[s], 0, held.shape[0] - PAGES)

    pl.semaphore_wait(barrier, n)
    msgs, pages, reps = [], [], []
    for s in range(1, n):
        c = pltpu.make_async_remote_copy(msg.at[s], msg_in.at[s], msg_ss.at[s], msg_rs.at[s],
                                         device_id=peer(-s), device_id_type=MESH)
        c.start()
        msgs.append(c)
        pages.append(pltpu.make_async_remote_copy(
            outbound.at[s], inbound.at[pl.ds(s * PAGES, PAGES)], page_ss.at[s], page_rs.at[s],
            device_id=peer(s), device_id_type=MESH))
        reps.append(pltpu.make_async_remote_copy(
            rep.at[s], rep_in.at[s], rep_ss.at[s], rep_rs.at[s],
            device_id=peer(s), device_id_type=MESH))
    load_held.wait()
    order = sorted(range(1, n), key=lambda s: abs(2 * s - n))
    for k, s in enumerate(order + [0]):
        for p in range(PAGES):
            outbound[s, p] = held[base_s[s] + p]
        if k < EARLY:
            pages[s - 1].start()

    loads = [
        pltpu.make_async_copy(src, dst, load_sem.at[i])
        for i, (src, dst) in enumerate([
            (pool.at[pl.ds(0, homes)], resident), (out_w, ow_v), (depth_in, di_v),
            (code_embed, ce_v), (depth_head, dh_v)])
    ]
    for c in loads:
        c.start()

    wide = jnp.concatenate([queries[...].astype(F32), kv32[:, 0, :], kv32[:, 1, :]], axis=1)
    for c in range(3 * heads):
        qkv3[:, c, :] = wide[:, c * HD:(c + 1) * HD]
    msg_in[0] = jnp.zeros_like(msg_in[0])
    rep_in[0] = jnp.zeros_like(rep_in[0])

    for c in msgs:
        c.wait_recv()

    @pl.loop(0, n // GROUP)
    def _(t):
        at = [t * GROUP + j for j in range(GROUP)]
        got = [msg_in[a].astype(F32) for a in at]
        out = attend_group(
            lambda j, p, kv: outbound[at[j], p, kv],
            [x[0:heads] for x in got], [x[heads:2 * heads] for x in got],
            [x[2 * heads:3 * heads] for x in got],
            [x[3 * heads:4 * heads, 0:1].astype(jnp.int32) for x in got])
        for j in range(GROUP):
            rep[at[j]] = out[j]

    for c in reps:
        c.start()
    for s in order[EARLY:]:
        pages[s - 1].start()

    loads[0].wait()

    @pl.loop(0, sessions // GROUP)
    def _(t):
        at = [t * GROUP + j for j in range(GROUP)]
        got = [qkv3[a] for a in at]
        out = attend_group(
            lambda j, p, kv: resident[at[j] * PAGES + p, kv],
            [x[0:heads] for x in got], [x[heads:2 * heads] for x in got],
            [x[2 * heads:3 * heads] for x in got], [lens[a] for a in at])
        for j in range(GROUP):
            local[at[j]] = out[j]

    for i in range(sessions):
        for h in range(2):
            settle(resident, (i * PAGES, i * PAGES + 1, i * PAGES + 2), h,
                   lens[i], kv32[i, h:h + 1, :], None)

    loads[3].wait()
    count, books = tokens.shape
    entries = code_embed.shape[0]
    diag = iota((books, books), 0) == iota((books, books), 1)
    picks = []
    for b in range(count):
        col = jnp.sum(jnp.where(diag, tokens[b:b + 1, :].astype(F32), 0.0), axis=1, keepdims=True)
        hit = col.astype(jnp.int32) == iota((books, entries), 1)
        picks.append(jnp.where(hit, 1.0, 0.0))
    pick = jnp.concatenate(picks, axis=0).astype(BF16)

    @pl.loop(0, emb.shape[1] // COLS)
    def _(t):
        at = pl.ds(pl.multiple_of(t * COLS, COLS), COLS)
        emb[:, at] = jnp.dot(pick, ce_v[:, at], preferred_element_type=F32)

    for c in reps:
        c.wait_recv()
    here = jnp.concatenate([local[:, h, :] for h in range(heads)], axis=1)
    away = jnp.concatenate([rep_in[:, h, :] for h in range(heads)], axis=1).astype(BF16)
    away = jnp.dot(pair.astype(BF16), away, preferred_element_type=F32)
    linked = jnp.sum(pair, axis=1, keepdims=True) > 0.0
    attention = jnp.where(linked, away, here).astype(BF16)

    loads[1].wait()

    def project(first, target):
        @pl.loop(0, half // COLS)
        def _(t):
            at = pl.ds(pl.multiple_of(first + t * COLS, COLS), COLS)
            to = pl.ds(pl.multiple_of(t * COLS, COLS), COLS)
            target[:, to] = jnp.dot(attention, ow_v[:, at], preferred_element_type=F32)

    def swap(i, src, dst):
        c = pltpu.make_async_remote_copy(src, dst, mp_ss.at[i], mp_rs.at[i],
                                         device_id=partner, device_id_type=MESH)
        c.start()
        return c

    project((1 - m) * half, po_send)
    swap0 = swap(0, po_send, po_in)
    project(m * half, po_mine)
    swap0.wait_recv()
    my_half = pl.ds(pl.multiple_of(m * half, half), half)
    layer = residual[:, my_half].astype(F32) + (po_mine[...] + po_in[...])
    layer = layer.astype(BF16).astype(F32)
    squares = jnp.sum(layer * layer, axis=1, keepdims=True)
    ss_send[...] = jnp.broadcast_to(squares, ss_send.shape)
    swap1 = swap(1, ss_send, ss_in)
    loads[2].wait()
    swap1.wait_recv()
    squares = squares + ss_in[:, 0:1]
    normed = (layer * lax.rsqrt(squares * (1.0 / features) + 1e-05) * norm_gain[:, my_half]).astype(BF16)
    for t in range(lf.shape[1] // COLS):
        at = slice(t * COLS, (t + 1) * COLS)
        lf[:, at] = jnp.dot(normed, di_v[:, at], preferred_element_type=F32)
    swap2 = swap(2, lf.at[pl.ds(pl.multiple_of((1 - m) * count, count), count)], lf_in)
    loads[4].wait()
    swap2.wait_recv()
    lifted = lf[pl.ds(pl.multiple_of(m * count, count), count), :] + lf_in[...]
    parts = []
    for b in range(count):
        hidden = lifted[b:b + 1, :] + emb[b * books:(b + 1) * books, :]
        mean = jnp.mean(hidden * hidden, axis=1, keepdims=True)
        parts.append(hidden * lax.rsqrt(mean + 1e-05) * depth_gain[...])
    depth_normed = jnp.concatenate(parts, axis=0).astype(BF16)
    for t in range(logits.shape[1] // COLS):
        at = slice(t * COLS, (t + 1) * COLS)
        logits[:, at] = jnp.dot(depth_normed, dh_v[:, at], preferred_element_type=F32).astype(BF16)

    for c in (swap0, swap1, swap2):
        c.wait_send()
    for c in msgs + reps:
        c.wait_send()
    for c in pages:
        c.wait_send()
    mine = jnp.where(rec_t[2:3, :] == me, rec_t[3:4, :], 0)
    total = jnp.sum(jnp.where(behind == iota((n, rows), 0), mine, 0).astype(F32), axis=1, keepdims=True)
    for s in order:
        pages[s - 1].wait_recv()
        for h in range(2):
            settle(inbound, tuple(s * PAGES + p for p in range(PAGES)), h,
                   sent_len_v[s:s + 1, 0:1].astype(jnp.int32),
                   sent_kv[s:s + 1, h * width:(h + 1) * width], total[s:s + 1].astype(jnp.int32))


def place_kernel(n, rec, resident, inbound, logits_in, cache, logits, sem, log_sem):
    me = lax.axis_index("dp")
    sessions = resident.shape[0] // PAGES
    copy_logits = pltpu.make_async_copy(logits_in, logits, log_sem)
    copy_logits.start()

    def from_holder(r, linked):
        mine = rec[2, r] == me
        i = rec[0, r] - me * sessions

        @pl.when(mine)
        def _():
            behind = me - rec[1, r]
            behind = jnp.where(behind < 0, behind + n, behind)
            pltpu.make_async_copy(inbound.at[pl.ds(behind * PAGES, PAGES)],
                                  cache.at[pl.ds(i * PAGES, PAGES)], sem).start()

        return tuple(jnp.where(mine & (i == j), 1, x) for j, x in enumerate(linked))

    linked = lax.fori_loop(0, rec.shape[1], from_holder, tuple(jnp.int32(0) for _ in range(sessions)))
    for i in range(sessions):
        @pl.when(linked[i] == 0)
        def _():
            pltpu.make_async_copy(resident.at[pl.ds(i * PAGES, PAGES)],
                                  cache.at[pl.ds(i * PAGES, PAGES)], sem).start()
    pltpu.make_async_copy(resident, cache, sem).wait()
    copy_logits.wait()


def on_device(n, residual, queries, new_kv, kv_pool, cache_len, reconnect, audio_tokens, out_weight,
              norm_gain, depth_in, code_embed, depth_gain, depth_head):
    sessions, width = queries.shape
    heads = width // HD
    count, books = audio_tokens.shape
    page = kv_pool.shape[1:]
    homes = sessions * PAGES
    features = residual.shape[1]
    half = features // 2
    depth = depth_in.shape[1]
    entries = depth_head.shape[1]
    vmem = pl.BlockSpec(memory_space=pltpu.VMEM)
    smem = pl.BlockSpec(memory_space=pltpu.SMEM)
    anywhere = pl.BlockSpec(memory_space=pltpu.HBM)
    dma = pltpu.SemaphoreType.DMA
    rec_t = reconnect.T
    inputs = (rec_t, cache_len.reshape(1, sessions), queries, new_kv, residual, audio_tokens,
              norm_gain.reshape(1, features), depth_gain.reshape(1, depth))
    def stay(x):
        return pltpu.with_memory_space_constraint(x, pltpu.HBM)

    inputs = tuple(stay(x) for x in inputs)
    large = tuple(stay(x) for x in (kv_pool, out_weight, depth_in, code_embed, depth_head))
    inbound, resident, logits = pl.pallas_call(
        functools.partial(main_kernel, n),
        out_shape=(jax.ShapeDtypeStruct((n * PAGES,) + page, BF16),
                   jax.ShapeDtypeStruct((homes,) + page, BF16),
                   jax.ShapeDtypeStruct((count * books, entries), BF16)),
        in_specs=[smem, smem] + [anywhere] * 13,
        out_specs=(vmem, vmem, vmem),
        scratch_shapes=[pltpu.VMEM(x.shape, x.dtype) for x in inputs] + [
            pltpu.VMEM((kv_pool.shape[0] - homes,) + page, BF16),
            pltpu.VMEM((n, PAGES) + page, BF16),
            pltpu.VMEM(out_weight.shape, BF16),
            pltpu.VMEM(depth_in.shape, BF16),
            pltpu.VMEM(code_embed.shape, BF16),
            pltpu.VMEM(depth_head.shape, BF16),
            pltpu.VMEM(new_kv.shape, F32),
            pltpu.VMEM((n, 2 * width), F32),
            pltpu.VMEM((n, HD), F32),
            dma((len(inputs),)),
            pltpu.VMEM((sessions, 3 * heads, HD), F32),
            pltpu.VMEM((n, 4 * heads, HD), F32),
            pltpu.VMEM((n, 4 * heads, HD), BF16),
            pltpu.VMEM((n, 4 * heads, HD), BF16),
            pltpu.VMEM((n, heads, HD), F32),
            pltpu.VMEM((n, heads, HD), F32),
            pltpu.VMEM((sessions, heads, HD), F32),
            pltpu.VMEM((sessions, half), F32),
            pltpu.VMEM((sessions, half), F32),
            pltpu.VMEM((sessions, half), F32),
            pltpu.VMEM((sessions, HD), F32),
            pltpu.VMEM((sessions, HD), F32),
            pltpu.VMEM((sessions, depth), F32),
            pltpu.VMEM((count, depth), F32),
            pltpu.VMEM((count * books, depth), F32),
            pltpu.SMEM((n,), jnp.int32),
            dma, dma((5,)), dma((n,)), dma((n,)), dma((n,)), dma((n,)), dma((n,)), dma((n,)),
            dma((3,)), dma((3,)),
        ],
        compiler_params=pltpu.CompilerParams(
            collective_id=0, has_side_effects=True, vmem_limit_bytes=32 * 1024 * 1024),
        name="serve",
    )(rec_t, cache_len, *inputs, *large)
    new_cache, logits = pl.pallas_call(
        functools.partial(place_kernel, n),
        out_shape=(jax.ShapeDtypeStruct((homes,) + page, BF16),
                   jax.ShapeDtypeStruct((count * books, entries), BF16)),
        in_specs=[smem, vmem, vmem, vmem],
        out_specs=(anywhere, anywhere),
        scratch_shapes=[dma, dma],
        compiler_params=pltpu.CompilerParams(vmem_limit_bytes=16 * 1024 * 1024),
        name="place",
    )(rec_t, resident, inbound, logits)
    return (logits.reshape(count, books, entries), new_cache)


def solution(mesh):
    in_specs = (
        P(("groups", "dp"), None),
        P(("groups", "dp"), "mp"),
        P(("groups", "dp"), None, "mp"),
        P(("groups", "dp"), None, None, "mp"),
        P(("groups", "dp")),
        P("groups", None),
        P(("groups", "dp", "mp"), None),
        P("mp", None),
        P(),
        P("mp", None),
        P(),
        P(),
        P(),
    )
    out_specs = (P(("groups", "dp", "mp"), None, None), P(("groups", "dp"), None, None, "mp"))
    return jax.shard_map(
        functools.partial(on_device, mesh.shape["dp"]), mesh=mesh, in_specs=in_specs,
        out_specs=out_specs, check_vma=False
    )
```

```python
import functools

import jax
import jax.numpy as jnp
from jax import lax
from jax.experimental import pallas as pl
from jax.experimental.pallas import tpu as pltpu
from jax.sharding import PartitionSpec as P

HD = 128
PAGES = 3
GROUP = 8
COLS = 512
EARLY = 1
F32 = jnp.float32
BF16 = jnp.bfloat16
MESH = pl.DeviceIdType.MESH


def iota(shape, dim):
    return lax.broadcasted_iota(jnp.int32, shape, dim)


def attend_group(pages_of, q8s, k8s, v8s, lens):
    heads = q8s[0].shape[0]
    width = heads * HD
    own = (iota((heads, width), 1) // HD) == iota((heads, width), 0)
    scores, heres = [], []
    for j in range(len(q8s)):
        keys = jnp.concatenate([pages_of(j, p, 0) for p in range(PAGES)], axis=0)
        place = iota((heads, keys.shape[0]), 1)
        spread = jnp.where(own, jnp.concatenate([q8s[j]] * heads, axis=1), 0.0).astype(BF16)
        s = lax.dot_general(spread, keys, (((1,), (1,)), ((), ())), preferred_element_type=F32)
        s = s * HD ** (-0.5)
        fresh = jnp.sum(q8s[j] * k8s[j], axis=1, keepdims=True) * HD ** (-0.5)
        here = place == lens[j]
        s = jnp.where(here, fresh, s)
        scores.append(jnp.where(place <= lens[j], s, -jnp.inf))
        heres.append(here)
    s = jnp.concatenate(scores, axis=0)
    e = jnp.exp(s - jnp.max(s, axis=1, keepdims=True))
    w = (e / jnp.sum(e, axis=1, keepdims=True)).astype(BF16).astype(F32)
    row = iota((heads, HD), 0)
    results = []
    for j in range(len(q8s)):
        mine = w[j * heads:(j + 1) * heads]
        values = jnp.concatenate([pages_of(j, p, 1) for p in range(PAGES)], axis=0)
        old = jnp.where(heres[j], 0.0, mine).astype(BF16)
        mixed = jnp.dot(old, values, preferred_element_type=F32)
        total = jnp.sum(jnp.where(heres[j], mine, 0.0), axis=1, keepdims=True) * v8s[j]
        for h in range(heads):
            total = total + jnp.where(row == h, mixed[:, h * HD:(h + 1) * HD], 0.0)
        results.append(total)
    return results


def settle(cache, pages, h, length, new, count):
    size, width = cache.shape[2:]
    for p, at in enumerate(pages):
        old = cache[at, h].astype(F32)
        if count is not None:
            old = jnp.where(p < count, old, 0.0)
        hit = iota((size, width), 0) + p * size == length
        cache[at, h] = jnp.where(hit, new, old).astype(BF16)


def main_kernel(n, rec, lens, *refs):
    small_in, (pool, out_w, depth_in, code_embed, depth_head), (inbound, resident, logits) = (
        refs[:8], refs[8:13], refs[13:16])
    rec_t, len_row, queries, kv, residual, tokens, norm_gain, depth_gain = small = refs[16:24]
    run_main(n, rec, lens, rec_t, len_row, queries, kv, residual, tokens, norm_gain, depth_gain,
             pool, out_w, depth_in, code_embed, depth_head, inbound, resident, logits,
             small_in, small, *refs[24:])


def run_main(n, rec, lens, rec_t, len_row, queries, kv, residual, tokens, norm_gain, depth_gain,
                pool, out_w, depth_in, code_embed, depth_head,
                inbound, resident, logits, small_in, small,
                held, outbound, ow_v, di_v, ce_v, dh_v, kv32, sent_kv, sent_len_v, small_sem,
                qkv3, msg32, msg, msg_in, rep, rep_in, local,
                po_send, po_mine, po_in, ss_send, ss_in, lf, lf_in, emb, base_s,
                held_sem, load_sem, msg_ss, msg_rs, page_ss, page_rs, rep_ss, rep_rs, mp_ss, mp_rs):
    g, me, m = lax.axis_index("groups"), lax.axis_index("dp"), lax.axis_index("mp")
    sessions = residual.shape[0]
    width = queries.shape[1]
    heads = width // HD
    homes = sessions * PAGES
    rows = rec_t.shape[1]
    half = residual.shape[1] // 2
    features = residual.shape[1]

    load_held = pltpu.make_async_copy(pool.at[pl.ds(homes, held.shape[0])], held, held_sem)
    load_held.start()
    fetch = [pltpu.make_async_copy(src, dst, small_sem.at[i])
             for i, (src, dst) in enumerate(zip(small_in, small))]
    for c in fetch:
        c.start()

    def peer(shift):
        return (g, lax.rem(me + shift + n, n), m)

    partner = (g, me, 1 - m)
    barrier = pltpu.get_barrier_semaphore()
    for s in range(1, n):
        pl.semaphore_signal(barrier, inc=1, device_id=peer(s), device_id_type=MESH)
    pl.semaphore_signal(barrier, inc=1, device_id=partner, device_id_type=MESH)

    for c in fetch:
        c.wait()
    kv32[...] = kv[...].astype(F32)

    session, holder = rec_t[0:1, :], rec_t[1:2, :]
    behind = me - holder
    behind = jnp.where(behind < 0, behind + n, behind)
    is_session = jnp.where(session == iota((sessions, rows), 0) + me * sessions, 1.0, 0.0).astype(BF16)
    is_slot = jnp.where(behind == iota((n, rows), 0), 1.0, 0.0).astype(BF16)
    nt = (((1,), (1,)), ((), ()))
    pair = lax.dot_general(is_session, is_slot, nt, preferred_element_type=F32)
    pair_t = lax.dot_general(is_slot, is_session, nt, preferred_element_type=F32).astype(BF16)
    eye = iota((sessions, sessions), 0) == iota((sessions, sessions), 1)
    len_col = jnp.sum(jnp.where(eye, len_row[...].astype(F32), 0.0), axis=1, keepdims=True)
    len_wide = jnp.broadcast_to(len_col, (sessions, HD)).astype(BF16)
    sent = jnp.concatenate(
        [jnp.dot(pair_t, x, preferred_element_type=F32)
         for x in (queries[...], kv32[:, 0, :].astype(BF16), kv32[:, 1, :].astype(BF16))], axis=1)
    sent_kv[...] = sent[:, width:]
    sent_len_v[...] = sent_len = jnp.dot(pair_t, len_wide, preferred_element_type=F32)
    for c in range(3 * heads):
        msg32[:, c, :] = sent[:, c * HD:(c + 1) * HD]
    for c in range(heads):
        msg32[:, 3 * heads + c, :] = sent_len
    msg[...] = msg32[...].astype(BF16)

    pl.semaphore_wait(barrier, n)
    msgs, pages, reps = [], [], []
    for s in range(1, n):
        c = pltpu.make_async_remote_copy(msg.at[s], msg_in.at[s], msg_ss.at[s], msg_rs.at[s],
                                         device_id=peer(-s), device_id_type=MESH)
        c.start()
        msgs.append(c)
        pages.append(pltpu.make_async_remote_copy(
            outbound.at[s], inbound.at[pl.ds(s * PAGES, PAGES)], page_ss.at[s], page_rs.at[s],
            device_id=peer(s), device_id_type=MESH))
        reps.append(pltpu.make_async_remote_copy(
            rep.at[s], rep_in.at[s], rep_ss.at[s], rep_rs.at[s],
            device_id=peer(s), device_id_type=MESH))
    def find(r, bases):
        ahead = rec[2, r] - me
        ahead = jnp.where(ahead < 0, ahead + n, ahead)
        ahead = jnp.where(rec[1, r] == me, ahead, -1)
        first = rec[4, r] - homes
        return tuple(jnp.where(ahead == s, first, b) for s, b in enumerate(bases))

    bases = lax.fori_loop(0, rows, find, tuple(jnp.int32(0) for _ in range(n)))
    for s in range(n):
        base_s[s] = jnp.clip(bases[s], 0, held.shape[0] - PAGES)

    load_held.wait()
    order = sorted(range(1, n), key=lambda s: abs(2 * s - n))
    for k, s in enumerate(order + [0]):
        for p in range(PAGES):
            outbound[s, p] = held[base_s[s] + p]
        if k < EARLY:
            pages[s - 1].start()

    loads = [
        pltpu.make_async_copy(src, dst, load_sem.at[i])
        for i, (src, dst) in enumerate([
            (pool.at[pl.ds(0, homes)], resident), (out_w, ow_v), (depth_in, di_v),
            (code_embed, ce_v), (depth_head, dh_v)])
    ]
    for c in loads:
        c.start()

    wide = jnp.concatenate([queries[...].astype(F32), kv32[:, 0, :], kv32[:, 1, :]], axis=1)
    for c in range(3 * heads):
        qkv3[:, c, :] = wide[:, c * HD:(c + 1) * HD]
    msg_in[0] = jnp.zeros_like(msg_in[0])
    rep_in[0] = jnp.zeros_like(rep_in[0])

    for c in msgs:
        c.wait_recv()

    @pl.loop(0, n // GROUP)
    def _(t):
        at = [t * GROUP + j for j in range(GROUP)]
        got = [msg_in[a].astype(F32) for a in at]
        out = attend_group(
            lambda j, p, kv: outbound[at[j], p, kv],
            [x[0:heads] for x in got], [x[heads:2 * heads] for x in got],
            [x[2 * heads:3 * heads] for x in got],
            [x[3 * heads:4 * heads, 0:1].astype(jnp.int32) for x in got])
        for j in range(GROUP):
            rep[at[j]] = out[j]

    for c in reps:
        c.start()
    for s in order[EARLY:]:
        pages[s - 1].start()

    loads[0].wait()

    @pl.loop(0, sessions // GROUP)
    def _(t):
        at = [t * GROUP + j for j in range(GROUP)]
        got = [qkv3[a] for a in at]
        out = attend_group(
            lambda j, p, kv: resident[at[j] * PAGES + p, kv],
            [x[0:heads] for x in got], [x[heads:2 * heads] for x in got],
            [x[2 * heads:3 * heads] for x in got], [lens[a] for a in at])
        for j in range(GROUP):
            local[at[j]] = out[j]

    for i in range(sessions):
        for h in range(2):
            settle(resident, (i * PAGES, i * PAGES + 1, i * PAGES + 2), h,
                   lens[i], kv32[i, h:h + 1, :], None)

    loads[3].wait()
    count, books = tokens.shape
    entries = code_embed.shape[0]
    diag = iota((books, books), 0) == iota((books, books), 1)
    picks = []
    for b in range(count):
        col = jnp.sum(jnp.where(diag, tokens[b:b + 1, :].astype(F32), 0.0), axis=1, keepdims=True)
        hit = col.astype(jnp.int32) == iota((books, entries), 1)
        picks.append(jnp.where(hit, 1.0, 0.0))
    pick = jnp.concatenate(picks, axis=0).astype(BF16)

    @pl.loop(0, emb.shape[1] // COLS)
    def _(t):
        at = pl.ds(pl.multiple_of(t * COLS, COLS), COLS)
        emb[:, at] = jnp.dot(pick, ce_v[:, at], preferred_element_type=F32)

    for c in reps:
        c.wait_recv()
    here = jnp.concatenate([local[:, h, :] for h in range(heads)], axis=1)
    away = jnp.concatenate([rep_in[:, h, :] for h in range(heads)], axis=1).astype(BF16)
    away = jnp.dot(pair.astype(BF16), away, preferred_element_type=F32)
    linked = jnp.sum(pair, axis=1, keepdims=True) > 0.0
    attention = jnp.where(linked, away, here).astype(BF16)

    loads[1].wait()

    def project(first, target):
        @pl.loop(0, half // COLS)
        def _(t):
            at = pl.ds(pl.multiple_of(first + t * COLS, COLS), COLS)
            to = pl.ds(pl.multiple_of(t * COLS, COLS), COLS)
            target[:, to] = jnp.dot(attention, ow_v[:, at], preferred_element_type=F32)

    def swap(i, src, dst):
        c = pltpu.make_async_remote_copy(src, dst, mp_ss.at[i], mp_rs.at[i],
                                         device_id=partner, device_id_type=MESH)
        c.start()
        return c

    project((1 - m) * half, po_send)
    swap0 = swap(0, po_send, po_in)
    project(m * half, po_mine)
    swap0.wait_recv()
    my_half = pl.ds(pl.multiple_of(m * half, half), half)
    layer = residual[:, my_half].astype(F32) + (po_mine[...] + po_in[...])
    layer = layer.astype(BF16).astype(F32)
    squares = jnp.sum(layer * layer, axis=1, keepdims=True)
    ss_send[...] = jnp.broadcast_to(squares, ss_send.shape)
    swap1 = swap(1, ss_send, ss_in)
    loads[2].wait()
    swap1.wait_recv()
    squares = squares + ss_in[:, 0:1]
    normed = (layer * lax.rsqrt(squares * (1.0 / features) + 1e-05) * norm_gain[:, my_half]).astype(BF16)
    for t in range(lf.shape[1] // COLS):
        at = slice(t * COLS, (t + 1) * COLS)
        lf[:, at] = jnp.dot(normed, di_v[:, at], preferred_element_type=F32)
    swap2 = swap(2, lf.at[pl.ds(pl.multiple_of((1 - m) * count, count), count)], lf_in)
    loads[4].wait()
    swap2.wait_recv()
    lifted = lf[pl.ds(pl.multiple_of(m * count, count), count), :] + lf_in[...]
    parts = []
    for b in range(count):
        hidden = lifted[b:b + 1, :] + emb[b * books:(b + 1) * books, :]
        mean = jnp.mean(hidden * hidden, axis=1, keepdims=True)
        parts.append(hidden * lax.rsqrt(mean + 1e-05) * depth_gain[...])
    depth_normed = jnp.concatenate(parts, axis=0).astype(BF16)
    for t in range(logits.shape[1] // COLS):
        at = slice(t * COLS, (t + 1) * COLS)
        logits[:, at] = jnp.dot(depth_normed, dh_v[:, at], preferred_element_type=F32).astype(BF16)

    for c in (swap0, swap1, swap2):
        c.wait_send()
    for c in msgs + reps:
        c.wait_send()
    for c in pages:
        c.wait_send()
    mine = jnp.where(rec_t[2:3, :] == me, rec_t[3:4, :], 0)
    total = jnp.sum(jnp.where(behind == iota((n, rows), 0), mine, 0).astype(F32), axis=1, keepdims=True)
    for s in order:
        pages[s - 1].wait_recv()
        for h in range(2):
            settle(inbound, tuple(s * PAGES + p for p in range(PAGES)), h,
                   sent_len_v[s:s + 1, 0:1].astype(jnp.int32),
                   sent_kv[s:s + 1, h * width:(h + 1) * width], total[s:s + 1].astype(jnp.int32))


def place_kernel(n, rec, resident, inbound, logits_in, cache, logits, sem, log_sem):
    me = lax.axis_index("dp")
    sessions = resident.shape[0] // PAGES
    copy_logits = pltpu.make_async_copy(logits_in, logits, log_sem)
    copy_logits.start()

    def from_holder(r, linked):
        mine = rec[2, r] == me
        i = rec[0, r] - me * sessions

        @pl.when(mine)
        def _():
            behind = me - rec[1, r]
            behind = jnp.where(behind < 0, behind + n, behind)
            pltpu.make_async_copy(inbound.at[pl.ds(behind * PAGES, PAGES)],
                                  cache.at[pl.ds(i * PAGES, PAGES)], sem).start()

        return tuple(jnp.where(mine & (i == j), 1, x) for j, x in enumerate(linked))

    linked = lax.fori_loop(0, rec.shape[1], from_holder, tuple(jnp.int32(0) for _ in range(sessions)))
    for i in range(sessions):
        @pl.when(linked[i] == 0)
        def _():
            pltpu.make_async_copy(resident.at[pl.ds(i * PAGES, PAGES)],
                                  cache.at[pl.ds(i * PAGES, PAGES)], sem).start()
    pltpu.make_async_copy(resident, cache, sem).wait()
    copy_logits.wait()


def on_device(n, residual, queries, new_kv, kv_pool, cache_len, reconnect, audio_tokens, out_weight,
              norm_gain, depth_in, code_embed, depth_gain, depth_head):
    sessions, width = queries.shape
    heads = width // HD
    count, books = audio_tokens.shape
    page = kv_pool.shape[1:]
    homes = sessions * PAGES
    features = residual.shape[1]
    half = features // 2
    depth = depth_in.shape[1]
    entries = depth_head.shape[1]
    vmem = pl.BlockSpec(memory_space=pltpu.VMEM)
    smem = pl.BlockSpec(memory_space=pltpu.SMEM)
    anywhere = pl.BlockSpec(memory_space=pltpu.HBM)
    dma = pltpu.SemaphoreType.DMA
    rec_t = reconnect.T
    inputs = (rec_t, cache_len.reshape(1, sessions), queries, new_kv, residual, audio_tokens,
              norm_gain.reshape(1, features), depth_gain.reshape(1, depth))
    def stay(x):
        return pltpu.with_memory_space_constraint(x, pltpu.HBM)

    inputs = tuple(stay(x) for x in inputs)
    large = tuple(stay(x) for x in (kv_pool, out_weight, depth_in, code_embed, depth_head))
    inbound, resident, logits = pl.pallas_call(
        functools.partial(main_kernel, n),
        out_shape=(jax.ShapeDtypeStruct((n * PAGES,) + page, BF16),
                   jax.ShapeDtypeStruct((homes,) + page, BF16),
                   jax.ShapeDtypeStruct((count * books, entries), BF16)),
        in_specs=[smem, smem] + [anywhere] * 13,
        out_specs=(vmem, vmem, vmem),
        scratch_shapes=[pltpu.VMEM(x.shape, x.dtype) for x in inputs] + [
            pltpu.VMEM((kv_pool.shape[0] - homes,) + page, BF16),
            pltpu.VMEM((n, PAGES) + page, BF16),
            pltpu.VMEM(out_weight.shape, BF16),
            pltpu.VMEM(depth_in.shape, BF16),
            pltpu.VMEM(code_embed.shape, BF16),
            pltpu.VMEM(depth_head.shape, BF16),
            pltpu.VMEM(new_kv.shape, F32),
            pltpu.VMEM((n, 2 * width), F32),
            pltpu.VMEM((n, HD), F32),
            dma((len(inputs),)),
            pltpu.VMEM((sessions, 3 * heads, HD), F32),
            pltpu.VMEM((n, 4 * heads, HD), F32),
            pltpu.VMEM((n, 4 * heads, HD), BF16),
            pltpu.VMEM((n, 4 * heads, HD), BF16),
            pltpu.VMEM((n, heads, HD), F32),
            pltpu.VMEM((n, heads, HD), F32),
            pltpu.VMEM((sessions, heads, HD), F32),
            pltpu.VMEM((sessions, half), F32),
            pltpu.VMEM((sessions, half), F32),
            pltpu.VMEM((sessions, half), F32),
            pltpu.VMEM((sessions, HD), F32),
            pltpu.VMEM((sessions, HD), F32),
            pltpu.VMEM((sessions, depth), F32),
            pltpu.VMEM((count, depth), F32),
            pltpu.VMEM((count * books, depth), F32),
            pltpu.SMEM((n,), jnp.int32),
            dma, dma((5,)), dma((n,)), dma((n,)), dma((n,)), dma((n,)), dma((n,)), dma((n,)),
            dma((3,)), dma((3,)),
        ],
        compiler_params=pltpu.CompilerParams(
            collective_id=0, has_side_effects=True, vmem_limit_bytes=32 * 1024 * 1024),
        name="serve",
    )(rec_t, cache_len, *inputs, *large)
    new_cache, logits = pl.pallas_call(
        functools.partial(place_kernel, n),
        out_shape=(jax.ShapeDtypeStruct((homes,) + page, BF16),
                   jax.ShapeDtypeStruct((count * books, entries), BF16)),
        in_specs=[smem, vmem, vmem, vmem],
        out_specs=(anywhere, anywhere),
        scratch_shapes=[dma, dma],
        compiler_params=pltpu.CompilerParams(vmem_limit_bytes=16 * 1024 * 1024),
        name="place",
    )(rec_t, resident, inbound, logits)
    return (logits.reshape(count, books, entries), new_cache)


def solution(mesh):
    in_specs = (
        P(("groups", "dp"), None),
        P(("groups", "dp"), "mp"),
        P(("groups", "dp"), None, "mp"),
        P(("groups", "dp"), None, None, "mp"),
        P(("groups", "dp")),
        P("groups", None),
        P(("groups", "dp", "mp"), None),
        P("mp", None),
        P(),
        P("mp", None),
        P(),
        P(),
        P(),
    )
    out_specs = (P(("groups", "dp", "mp"), None, None), P(("groups", "dp"), None, None, "mp"))
    return jax.shard_map(
        functools.partial(on_device, mesh.shape["dp"]), mesh=mesh, in_specs=in_specs,
        out_specs=out_specs, check_vma=False
    )
```
